768 devices in a mesh: dp: 48 (over z, y_hi, core), tensor: 16 (over y_lo, x).
Axes of the slice: x: 4, y: 8 (y_hi: 2, y_lo: 4; y = y_hi * 4 + y_lo), z: 12, core: 2. Of those that a mesh axis runs over, the one named last changes fastest.
Arguments:
- hidden: bfloat16 [6144, 14336], P('dp', 'tensor'), may hold values from -6 to 6
- down_weight: bfloat16 [4096, 14336], P(None, 'tensor'), may hold values from -0.046875 to 0.046875
- encoder: bfloat16 [4096, 768], P(None, 'dp'), may hold values from -0.09375 to 0.09375
- decoder: bfloat16 [768, 4096], P(None, 'tensor'), may hold values from -0.21875 to 0.21875
- cotangent: bfloat16 [6144, 4096], P('dp', 'tensor'), may hold values from -6 to 6
Outputs:
- output: bfloat16 [6144, 4096], P('dp', 'tensor')
- grad_hidden: bfloat16 [6144, 14336], P('dp', 'tensor')
- grad_decoder: float32 [768, 4096], P('dp', 'tensor')
The draws below stay inside these ranges and needn't reach their ends.
All inputs are finite; a program needn't handle non-finite values.
Results may differ from the reference program's by a relative error of at most 0.0057.
Values may be sent and summed in bfloat16 or wider, within the bound.
A program may use at most 64 MiB of HBM per device.

```python
import jax
import jax.numpy as jnp
from jax import lax

D = 4096
L = 768
FF_DEV = 896
FF = 14336
TOKENS = 6144
N_TENSOR = 16


def level_of(stream_key, dims, shards, low, high):
    def one(axis_at, blocks):
        heights = jax.random.uniform(jax.random.fold_in(jax.random.fold_in(stream_key, 6), axis_at), (blocks,), jnp.float32, low / len(shards), high / len(shards))
        return jnp.repeat(jnp.exp(heights), dims[axis_at] // blocks).reshape((-1,) + (1,) * (len(dims) - axis_at - 1))

    gain = one(*shards[0])
    for cut in shards[1:]:
        gain = gain * one(*cut)
    return gain


def noise(key, dims, spread, reach, cuts=(), kind=jnp.bfloat16):
    values = jax.random.normal(key, dims, jnp.float32) * spread
    if len(cuts) > 0:
        values = level_of(key, dims, cuts, -0.22, 0.18) * values
    return jnp.clip(values, min=-reach, max=reach).astype(kind)


def setup_inputs(seed: int = 0) -> dict:
    keys = jax.random.split(jax.random.key(seed), 6)
    return {
        "hidden": noise(keys[0], (TOKENS, FF), 1.0, 6.0, ((0, 48), (1, 16))),
        "down_weight": noise(keys[1], (D, FF), FF ** -0.5, 0.046875, ((1, 16),)),
        "encoder": noise(keys[2], (D, L), D ** -0.5, 0.09375, ((1, 48),)),
        "decoder": noise(keys[3], (L, D), L ** -0.5, 0.21875, ((1, 16),)),
        "cotangent": noise(keys[4], (TOKENS, D), 1.0, 6.0, ((0, 48), (1, 16))),
    }


def reference(hidden, down_weight, encoder, decoder, cotangent):

    def accumulate(summed, index):
        lower = (index * FF_DEV).astype(jnp.int32)
        block_hidden = lax.dynamic_slice_in_dim(hidden, lower, FF_DEV, 1)
        block_weight = lax.dynamic_slice_in_dim(down_weight, lower, FF_DEV, 1)
        partial_value = lax.dot_general(block_hidden, block_weight, (((1,), (1,)), ((), ())), preferred_element_type=jnp.float32).astype(jnp.bfloat16)
        return (summed + jnp.dot(partial_value, encoder, preferred_element_type=jnp.float32), None)
    start_sum = jnp.zeros((TOKENS, L), jnp.float32)
    latent, unused = lax.scan(accumulate, start_sum, jnp.arange(N_TENSOR, dtype=jnp.int32))
    shared = latent.astype(jnp.bfloat16)
    output = jnp.dot(shared, decoder, preferred_element_type=jnp.float32).astype(jnp.bfloat16)
    grad_decoder = lax.dot_general(shared, cotangent, (((0,), (0,)), ((), ())), preferred_element_type=jnp.float32)
    grad_decoder = grad_decoder * (1.0 / math_sqrt(TOKENS))
    grad_latent = lax.dot_general(cotangent, decoder, (((1,), (1,)), ((), ())), preferred_element_type=jnp.float32).astype(jnp.bfloat16)
    grad_partial = lax.dot_general(grad_latent, encoder, (((1,), (1,)), ((), ())), preferred_element_type=jnp.float32).astype(jnp.bfloat16)
    grad_hidden = jnp.dot(grad_partial, down_weight, preferred_element_type=jnp.float32).astype(jnp.bfloat16)
    return (output, grad_hidden, grad_decoder)

def math_sqrt(value):
    return float(value) ** 0.5
```

```python
import jax
import jax.numpy as jnp
from jax import lax
from jax.experimental import pallas as pl
from jax.experimental.pallas import tpu as pltpu
from jax.sharding import PartitionSpec as P

MESH = pl.DeviceIdType.MESH
F32, BF16 = jnp.float32, jnp.bfloat16
NZ, NT = 12, 16
NP = 2 * NZ
ROWS = 48
HUBS = (3, NZ - 3, 6)
CHUNKS = 8


def nt(a, b):
    return lax.dot_general(a, b, (((1,), (1,)), ((), ())), preferred_element_type=F32)


def nn(a, b):
    return jnp.dot(a, b, preferred_element_type=F32)


def tn(a, b):
    return lax.dot_general(a, b, (((0,), (0,)), ((), ())), preferred_element_type=F32)


def kernel(
    h_hbm, dw_hbm, enc_hbm, dec_hbm, cot_hbm,
    out_ref, gh_ref, gd_ref,
    dwv, encv, decv, cotv, hv, mv,
    gterm, gslot, gfull, gsib,
    sterm, sslot, sfull, ssib,
    dterm, dslot,
    lsem, wsem, msend, mrecv, psend, precv, asend, arecv,
):
    dp, t = lax.axis_index("dp"), lax.axis_index("tensor")
    z, yh, c = dp // 4, (dp // 2) % 2, dp % 2
    place = z * 2 + yh

    def device(zz, yy):
        return ((zz * 2 + yy) * 2 + c, t)

    sibling = (dp + 1 - 2 * c, t)

    def along(k):
        return lax.rem(z + (k % NZ), NZ)

    depth = dw_hbm.shape[0] // CHUNKS
    own = [
        pltpu.make_async_copy(enc_hbm, encv, lsem.at[0]),
        pltpu.make_async_copy(cot_hbm, cotv.at[c], lsem.at[1]),
        pltpu.make_async_copy(h_hbm, hv.at[c], lsem.at[2]),
        pltpu.make_async_copy(dec_hbm.at[:, 0], decv.at[0], lsem.at[3]),
        pltpu.make_async_copy(dec_hbm.at[:, 1], decv.at[1], lsem.at[4]),
    ]
    weights = [
        pltpu.make_async_copy(
            dw_hbm.at[pl.ds(i * depth, depth)], dwv.at[pl.ds(i * depth, depth)], wsem.at[i]
        )
        for i in range(CHUNKS)
    ]
    own[0].start()
    for copy in weights[:2]:
        copy.start()
    for copy in own[1:]:
        copy.start()
    for copy in weights[2:]:
        copy.start()

    barrier = pltpu.get_barrier_semaphore()
    greet = [sibling, device(z, 1 - yh), device(along(1), yh), device(along(-1), yh)]
    greet += [device(along(k), yh) for k in HUBS]
    for who in greet:
        pl.semaphore_signal(barrier, inc=1, device_id=who, device_id_type=MESH)

    @pl.loop(1, NT)
    def _(k):
        pl.semaphore_signal(
            barrier, inc=1, device_id=(dp, lax.rem(t + k, NT)), device_id_type=MESH
        )

    own[0].wait()
    code = jnp.zeros((16, dwv.shape[1]), F32)
    for i in range(CHUNKS):
        cut = pl.ds(i * depth, depth)
        weights[i].wait()
        code += nn(encv[:, cut], dwv[cut, :])
    mv[c, place] = code.astype(BF16)
    for copy in own[1:]:
        copy.wait()

    pl.semaphore_wait(barrier, len(greet) + NT - 1)

    sent = []

    def pass_on(zz, yy, to):
        slot = zz * 2 + yy
        copy = pltpu.make_async_remote_copy(
            src_ref=mv.at[c, slot],
            dst_ref=mv.at[c, slot],
            send_sem=msend.at[len(sent)],
            recv_sem=mrecv.at[slot],
            device_id=to,
            device_id_type=MESH,
        )
        copy.start()
        sent.append(copy)

    def arrived(zz, yy):
        slot = zz * 2 + yy
        pltpu.make_async_copy(mv.at[c, slot], mv.at[c, slot], mrecv.at[slot]).wait()

    def pass_near(zz, yy):
        pass_on(zz, yy, device(along(1), yh))
        pass_on(zz, yy, device(along(-1), yh))

    pairs = []

    def to_sibling(src, dst):
        i = len(pairs)
        copy = pltpu.make_async_remote_copy(
            src_ref=src, dst_ref=dst, send_sem=psend.at[i], recv_sem=precv.at[i],
            device_id=sibling, device_id_type=MESH,
        )
        copy.start()
        pairs.append(copy)
        return copy

    def scatter(term, slots, i):
        @pl.loop(1, NT)
        def _(k):
            who = lax.rem(t + k, NT)
            pltpu.make_async_remote_copy(
                src_ref=term.at[who], dst_ref=slots.at[k - 1],
                send_sem=asend.at[i], recv_sem=arecv.at[i],
                device_id=(dp, who), device_id_type=MESH,
            ).start()

    def gather(full, i):
        @pl.loop(1, NT)
        def _(k):
            pltpu.make_async_remote_copy(
                src_ref=full.at[t], dst_ref=full.at[t],
                send_sem=asend.at[i], recv_sem=arecv.at[i],
                device_id=(dp, lax.rem(t + k, NT)), device_id_type=MESH,
            ).start()

    def all_of(ref, sem):
        pltpu.make_async_copy(ref, ref, sem).wait()

    def summed(term, slots):
        total = term[t].astype(F32)
        for k in range(NT - 1):
            total += slots[k].astype(F32)
        return total.astype(BF16)

    def split(term, value):
        for r in range(NT // 2):
            for s in range(2):
                term[2 * r + s] = value[r * ROWS:(r + 1) * ROWS, s * 128:(s + 1) * 128].astype(BF16)

    for k in HUBS:
        pass_on(z, yh, device(along(k), yh))
    pass_on(z, yh, device(z, 1 - yh))
    pass_near(z, yh)
    cot_pair = to_sibling(cotv.at[c], cotv.at[c])
    hid_pair = to_sibling(hv.at[c], hv.at[c])

    cot_pair.wait_recv()
    cot_both = cotv[...].reshape(-1, cotv.shape[2])
    split(gterm, nt(decv[c].reshape(-1, decv.shape[3]), cot_both))
    scatter(gterm, gslot, 0)

    arrived(z, 1 - yh)
    pass_near(z, 1 - yh)
    for k in HUBS:
        arrived(along(k), yh)
        pass_on(along(k), yh, device(z, 1 - yh))
        pass_near(along(k), yh)

    all_of(gslot, arecv.at[0])
    gfull[t] = summed(gterm, gslot)
    gather(gfull, 1)

    for k in HUBS:
        arrived(along(k), 1 - yh)
        pass_near(along(k), 1 - yh)
    for side in (1, -1):
        for k in (0,) + HUBS:
            for yy in range(2):
                arrived(along(side + k), yy)

    m_pair = to_sibling(mv.at[c], mv.at[c])
    hid_pair.wait_recv()
    width = hv.shape[2]
    split(sterm, nt(mv[c].reshape(-1, width), hv[...].reshape(-1, width)))
    scatter(sterm, sslot, 2)

    def own_tokens(full):
        return jnp.concatenate([full[2 * r + c] for r in range(NT // 2)], axis=0)

    def swap(full, sib):
        copies = []
        for r in range(NT // 2):
            copies.append(to_sibling(full.at[2 * r + 1 - c], sib.at[r]))
        return copies

    all_of(gfull.at[pl.ds(0, NT - 1)], arecv.at[1])
    g_swap = swap(gfull, gsib)
    m_pair.wait_recv()
    for copy in g_swap:
        copy.wait_recv()
    gh = tn(own_tokens(gfull), mv[c].reshape(-1, width))
    gh += tn(gsib[...].reshape(-1, 128), mv[1 - c].reshape(-1, width))
    gh_ref[...] = gh.astype(BF16)

    all_of(sslot, arecv.at[2])
    sfull[t] = summed(sterm, sslot)
    gather(sfull, 3)
    all_of(sfull.at[pl.ds(0, NT - 1)], arecv.at[3])

    left = jnp.concatenate([sfull[2 * r] for r in range(NT // 2)], axis=0)
    right = jnp.concatenate([sfull[2 * r + 1] for r in range(NT // 2)], axis=0)
    gd = nn(left, cotv[0]) + nn(right, cotv[1])
    dterm[...] = gd.astype(BF16).reshape(dterm.shape)

    @pl.loop(1, NP)
    def _(k):
        who = lax.rem(place + k, NP)
        pltpu.make_async_remote_copy(
            src_ref=dterm.at[who], dst_ref=dslot.at[k - 1],
            send_sem=asend.at[4], recv_sem=arecv.at[4],
            device_id=(who * 2 + c, t), device_id_type=MESH,
        ).start()

    s_swap = swap(sfull, ssib)
    for copy in s_swap:
        copy.wait_recv()
    value = tn(own_tokens(sfull), decv[c].reshape(-1, decv.shape[3]))
    value += tn(ssib[...].reshape(-1, 128), decv[1 - c].reshape(-1, decv.shape[3]))
    out_ref[...] = value.astype(BF16)

    all_of(dslot, arecv.at[4])
    total = dterm[place].astype(F32)
    for k in range(NP - 1):
        total += dslot[k].astype(F32)
    gd_ref[...] = total * (1.0 / 6144.0**0.5)

    for copy in sent:
        copy.wait_send()
    for copy in pairs:
        copy.wait_send()
    for i, ref in enumerate((gslot, gslot, gslot, gslot, dslot)):
        all_of(ref, asend.at[i])


def write_out(a, b, c, a_out, b_out, c_out, sem):
    copies = [
        pltpu.make_async_copy(src, dst, sem.at[i])
        for i, (src, dst) in enumerate(((a, a_out), (b, b_out), (c, c_out)))
    ]
    for copy in copies:
        copy.start()
    for copy in copies:
        copy.wait()


def per_device(hidden, down_weight, encoder, decoder, cotangent):
    tokens, width = hidden.shape
    model = down_weight.shape[0]
    wide = decoder.shape[1]
    hbm = pl.BlockSpec(memory_space=pltpu.HBM)
    vmem = pl.BlockSpec(memory_space=pltpu.VMEM)
    V, D = pltpu.VMEM, pltpu.SemaphoreType.DMA

    def exchange():
        return [
            V((NT, ROWS, 128), BF16),
            V((NT - 1, ROWS, 128), BF16),
            V((NT, ROWS, 128), BF16),
            V((NT // 2, ROWS, 128), BF16),
        ]

    results = pl.pallas_call(
        kernel,
        out_shape=(
            jax.ShapeDtypeStruct((tokens, wide), BF16),
            jax.ShapeDtypeStruct((tokens, width), BF16),
            jax.ShapeDtypeStruct((16, wide), F32),
        ),
        in_specs=[hbm] * 5,
        out_specs=(vmem, vmem, vmem),
        scratch_shapes=[
            V((model, width), BF16),
            V((16, model), BF16),
            V((2, NP, 16, wide), BF16),
            V((2, tokens, wide), BF16),
            V((2, tokens, width), BF16),
            V((2, NP, 16, width), BF16),
            *exchange(),
            *exchange(),
            V((NP, 16, wide), BF16),
            V((NP - 1, 16, wide), BF16),
            D((5,)), D((CHUNKS,)), D((NP - 1,)), D((NP,)), D((19,)), D((19,)), D((5,)), D((5,)),
        ],
        compiler_params=pltpu.CompilerParams(
            collective_id=0, has_side_effects=True, vmem_limit_bytes=56 * 2**20
        ),
        name="down_projection",
    )(hidden, down_weight, encoder.T, decoder.reshape(NP, 2, 16, wide), cotangent)

    return pl.pallas_call(
        write_out,
        out_shape=tuple(jax.ShapeDtypeStruct(r.shape, r.dtype) for r in results),
        in_specs=[vmem] * 3,
        out_specs=(hbm, hbm, hbm),
        scratch_shapes=[D((3,))],
        name="write_out",
    )(*results)


def solution(mesh):
    in_specs = (
        P("dp", "tensor"),
        P(None, "tensor"),
        P(None, "dp"),
        P(None, "tensor"),
        P("dp", "tensor"),
    )
    out_specs = (P("dp", "tensor"), P("dp", "tensor"), P("dp", "tensor"))
    return jax.shard_map(
        per_device, mesh=mesh, in_specs=in_specs, out_specs=out_specs, check_vma=False
    )
```

```python
import jax
import jax.numpy as jnp
from jax import lax
from jax.experimental import pallas as pl
from jax.experimental.pallas import tpu as pltpu
from jax.sharding import PartitionSpec as P

MESH = pl.DeviceIdType.MESH
F32, BF16 = jnp.float32, jnp.bfloat16
NZ, NT = 12, 16
NP = 2 * NZ
PARTS = 3
STEP = NP // PARTS
CHUNKS = 8


def nt(a, b):
    return lax.dot_general(a, b, (((1,), (1,)), ((), ())), preferred_element_type=F32)


def nn(a, b):
    return jnp.dot(a, b, preferred_element_type=F32)


def tn(a, b):
    return lax.dot_general(a, b, (((0,), (0,)), ((), ())), preferred_element_type=F32)


def flat(x):
    return x.reshape(-1, x.shape[-1])


def kernel(
    h_hbm, dw_hbm, enc_hbm, dec_hbm, cot_hbm,
    out_hbm, gh_hbm, gd_hbm,
    dwv, encv, decv, cotv, hv, mv,
    gterm, gslot, gfull, gsib,
    sterm, sslot, sfull, ssib,
    dterm, dslot, outv, ghv, gdv,
    lsem, wsem, osem, msend, mrecv, psend, precv, asend, arecv,
):
    dp, t = lax.axis_index("dp"), lax.axis_index("tensor")
    z, yh, c = dp // 4, (dp // 2) % 2, dp % 2
    place = z * 2 + yh
    yo = 1 - yh

    def along(k):
        return lax.rem(z + (k + NZ) % NZ, NZ)

    def device(k, yy):
        return ((along(k) * 2 + yy) * 2 + c, t)

    sibling = (dp + 1 - 2 * c, t)

    depth = dw_hbm.shape[0] // CHUNKS
    own = [
        pltpu.make_async_copy(enc_hbm, encv, lsem.at[0]),
        pltpu.make_async_copy(cot_hbm, cotv.at[c], lsem.at[1]),
        pltpu.make_async_copy(h_hbm, hv.at[c], lsem.at[2]),
        pltpu.make_async_copy(dec_hbm.at[:, 0], decv.at[0], lsem.at[3]),
        pltpu.make_async_copy(dec_hbm.at[:, 1], decv.at[1], lsem.at[4]),
    ]
    weights = [
        pltpu.make_async_copy(
            dw_hbm.at[pl.ds(i * depth, depth)], dwv.at[pl.ds(i * depth, depth)], wsem.at[i]
        )
        for i in range(CHUNKS)
    ]
    own[0].start()
    for copy in weights:
        copy.start()
    for copy in own[1:]:
        copy.start()

    barrier = pltpu.get_barrier_semaphore()
    near = (1, -1, 2, -2)
    greet = [sibling, device(0, yo)]
    greet += [device(k, yh) for k in near]
    greet += [device(k, yh) for k in (4, -4)]
    for who in greet:
        pl.semaphore_signal(barrier, inc=1, device_id=who, device_id_type=MESH)

    @pl.loop(1, NT)
    def _(k):
        pl.semaphore_signal(
            barrier, inc=1, device_id=(dp, lax.rem(t + k, NT)), device_id_type=MESH
        )

    own[0].wait()
    code = jnp.zeros((16, dwv.shape[1]), F32)
    for i in range(CHUNKS):
        cut = pl.ds(i * depth, depth)
        weights[i].wait()
        code += nn(encv[:, cut], dwv[cut, :])
    mv[c, place] = code.astype(BF16)

    pl.semaphore_wait(barrier, len(greet) + NT - 1)

    sent = []

    def pass_on(slot, *to):
        for who in to:
            copy = pltpu.make_async_remote_copy(
                src_ref=mv.at[c, slot], dst_ref=mv.at[c, slot],
                send_sem=msend.at[len(sent)], recv_sem=mrecv.at[slot],
                device_id=who, device_id_type=MESH,
            )
            copy.start()
            sent.append(copy)

    def arrived(slot):
        pltpu.make_async_copy(mv.at[c, slot], mv.at[c, slot], mrecv.at[slot]).wait()

    pairs = []

    def to_sibling(src, dst):
        i = len(pairs)
        copy = pltpu.make_async_remote_copy(
            src_ref=src, dst_ref=dst, send_sem=psend.at[i], recv_sem=precv.at[i],
            device_id=sibling, device_id_type=MESH,
        )
        copy.start()
        pairs.append(copy)
        return copy

    def scatter(term, slots, i):
        @pl.loop(1, NT)
        def _(k):
            who = lax.rem(t + k, NT)
            pltpu.make_async_remote_copy(
                src_ref=term.at[who], dst_ref=slots.at[k - 1],
                send_sem=asend.at[i], recv_sem=arecv.at[i],
                device_id=(dp, who), device_id_type=MESH,
            ).start()

    def gather(full, i):
        @pl.loop(1, NT)
        def _(k):
            pltpu.make_async_remote_copy(
                src_ref=full.at[t], dst_ref=full.at[t],
                send_sem=asend.at[i], recv_sem=arecv.at[i],
                device_id=(dp, lax.rem(t + k, NT)), device_id_type=MESH,
            ).start()

    def all_of(ref, sem):
        pltpu.make_async_copy(ref, ref, sem).wait()

    def reduce(term, slots, full, i):
        all_of(slots, arecv.at[i])
        total = term[t].astype(F32)
        for k in range(NT - 1):
            total += slots[k].astype(F32)
        full[t] = total.astype(BF16)
        gather(full, i + 1)

    def split(term, value):
        rows = value.shape[0] // 8
        for s in range(2):
            for r in range(8):
                term[8 * s + r] = value[r * rows:(r + 1) * rows, s * 128:(s + 1) * 128].astype(BF16)

    up, down = device(4, yh), device(-4, yh)
    one, two = (device(1, yh), device(-1, yh)), (device(2, yh), device(-2, yh))
    pass_on(place, up, down, device(0, yo), *one, *two)

    for copy in own[1:]:
        copy.wait()
    cot_pair = to_sibling(cotv.at[c], cotv.at[c])
    hid_pair = to_sibling(hv.at[c], hv.at[c])

    cot_pair.wait_recv()
    split(gterm, nt(flat(decv[c]), flat(cotv[...])))
    scatter(gterm, gslot, 0)

    turn = jnp.where(z // 4 == 1, NZ - 4, 4)
    first, second = lax.rem(z + turn, NZ) * 2, lax.rem(z + NZ - turn, NZ) * 2
    arrived(first + yh)
    pass_on(first + yh, device(0, yo), *one)
    arrived(z * 2 + yo)
    pass_on(z * 2 + yo, *one, *two)
    arrived(second + yh)
    pass_on(second + yh, device(0, yo), *one)
    pass_on(along(-4) * 2 + yh, two[0])
    arrived(first + yo)
    pass_on(first + yo, *one)
    arrived(second + yo)
    pass_on(second + yo, *one)
    pass_on(along(4) * 2 + yo, two[1])

    hid_pair.wait_recv()
    hidden_both = flat(hv[...])
    m_pairs = []

    def latent(n):
        for r in range(STEP // 2):
            @pl.when(lax.rem(z, 4) != r)
            def _():
                arrived(n * STEP + 2 * r)
                arrived(n * STEP + 2 * r + 1)

        rows = pl.ds(n * STEP, STEP)
        m_pairs.append(to_sibling(mv.at[c, rows], mv.at[c, rows]))
        split(sterm.at[n], nt(flat(mv[c, rows]), hidden_both))
        scatter(sterm.at[n], sslot.at[n], 2 + 2 * n)

    s_pairs = []

    def shared(n):
        all_of(sfull.at[n, pl.ds(0, NT - 1)], arecv.at[3 + 2 * n])
        s_pairs.append(to_sibling(sfull.at[n, pl.ds(8 * (1 - c), 8)], ssib.at[n]))

    def decoder_terms(n):
        gd = nn(flat(sfull[n, 0:8]), cotv[0]) + nn(flat(sfull[n, 8:16]), cotv[1])
        dterm[n * STEP:(n + 1) * STEP] = gd.astype(BF16).reshape(STEP, 16, -1)

        @pl.loop(n * STEP, (n + 1) * STEP)
        def _(who):
            @pl.when(who != place)
            def _():
                pltpu.make_async_remote_copy(
                    src_ref=dterm.at[who], dst_ref=dslot.at[lax.rem(who - place + NP, NP) - 1],
                    send_sem=asend.at[8], recv_sem=arecv.at[8],
                    device_id=(who * 2 + c, t), device_id_type=MESH,
                ).start()

    reduce(gterm, gslot, gfull, 0)
    latent(0)
    latent(1)
    reduce(sterm.at[0], sslot.at[0], sfull.at[0], 2)
    latent(2)
    reduce(sterm.at[1], sslot.at[1], sfull.at[1], 4)
    all_of(gfull.at[pl.ds(0, NT - 1)], arecv.at[1])
    g_pair = to_sibling(gfull.at[pl.ds(8 * (1 - c), 8)], gsib)
    shared(0)
    decoder_terms(0)
    reduce(sterm.at[2], sslot.at[2], sfull.at[2], 6)
    shared(1)
    decoder_terms(1)

    for copy in m_pairs:
        copy.wait_recv()
    g_pair.wait_recv()
    gh = tn(flat(gfull[pl.ds(8 * c, 8)]), flat(mv[c]))
    gh += tn(flat(gsib[...]), flat(mv[1 - c]))
    ghv[...] = gh.astype(BF16)
    gh_out = pltpu.make_async_copy(ghv, gh_hbm, osem.at[0])
    gh_out.start()

    shared(2)
    decoder_terms(2)
    for copy in s_pairs:
        copy.wait_recv()
    value = tn(flat(sfull[:, pl.ds(8 * c, 8)]), flat(decv[c]))
    value += tn(flat(ssib[...]), flat(decv[1 - c]))
    outv[...] = value.astype(BF16)
    out_out = pltpu.make_async_copy(outv, out_hbm, osem.at[1])
    out_out.start()

    all_of(dslot, arecv.at[8])
    total = dterm[place].astype(F32)
    for k in range(NP - 1):
        total += dslot[k].astype(F32)
    gdv[...] = total * (1.0 / 6144.0**0.5)
    gd_out = pltpu.make_async_copy(gdv, gd_hbm, osem.at[2])
    gd_out.start()

    for copy in sent:
        copy.wait_send()
    for copy in pairs:
        copy.wait_send()
    for i, ref in enumerate((gslot, gslot) + (sslot.at[0],) * 6 + (dslot,)):
        all_of(ref, asend.at[i])
    gh_out.wait()
    out_out.wait()
    gd_out.wait()


def write_out(a, b, c, a_out, b_out, c_out, sem):
    copies = [
        pltpu.make_async_copy(src, dst, sem.at[i])
        for i, (src, dst) in enumerate(((a, a_out), (b, b_out), (c, c_out)))
    ]
    for copy in copies:
        copy.start()
    for copy in copies:
        copy.wait()


def per_device(hidden, down_weight, encoder, decoder, cotangent):
    tokens, width = hidden.shape
    model = down_weight.shape[0]
    wide = decoder.shape[1]
    hbm = pl.BlockSpec(memory_space=pltpu.HBM)
    V, D = pltpu.VMEM, pltpu.SemaphoreType.DMA
    out_shape = (
        jax.ShapeDtypeStruct((tokens, wide), BF16),
        jax.ShapeDtypeStruct((tokens, width), BF16),
        jax.ShapeDtypeStruct((16, wide), F32),
    )

    results = pl.pallas_call(
        kernel,
        out_shape=out_shape,
        in_specs=[hbm] * 5,
        out_specs=(hbm,) * 3,
        scratch_shapes=[
            V((model, width), BF16),
            V((16, model), BF16),
            V((2, NP, 16, wide), BF16),
            V((2, tokens, wide), BF16),
            V((2, tokens, width), BF16),
            V((2, NP, 16, width), BF16),
            V((NT, 16 * PARTS, 128), BF16),
            V((NT - 1, 16 * PARTS, 128), BF16),
            V((NT, 16 * PARTS, 128), BF16),
            V((NT // 2, 16 * PARTS, 128), BF16),
            V((PARTS, NT, 16, 128), BF16),
            V((PARTS, NT - 1, 16, 128), BF16),
            V((PARTS, NT, 16, 128), BF16),
            V((PARTS, NT // 2, 16, 128), BF16),
            V((NP, 16, wide), BF16),
            V((NP - 1, 16, wide), BF16),
            V((tokens, wide), BF16),
            V((tokens, width), BF16),
            V((16, wide), F32),
            D((5,)), D((CHUNKS,)), D((3,)), D((NP - 1,)), D((NP,)), D((9,)), D((9,)), D((9,)), D((9,)),
        ],
        compiler_params=pltpu.CompilerParams(
            collective_id=0, has_side_effects=True, vmem_limit_bytes=56 * 2**20
        ),
        name="down_projection",
    )(hidden, down_weight, encoder.T, decoder.reshape(NP, 2, 16, wide), cotangent)

    return pl.pallas_call(
        write_out,
        out_shape=out_shape,
        in_specs=[pl.BlockSpec(memory_space=pltpu.VMEM)] * 3,
        out_specs=(hbm,) * 3,
        scratch_shapes=[D((3,))],
        name="write_out",
    )(*results)


def solution(mesh):
    in_specs = (
        P("dp", "tensor"),
        P(None, "tensor"),
        P(None, "dp"),
        P(None, "tensor"),
        P("dp", "tensor"),
    )
    out_specs = (P("dp", "tensor"), P("dp", "tensor"), P("dp", "tensor"))
    return jax.shard_map(
        per_device, mesh=mesh, in_specs=in_specs, out_specs=out_specs, check_vma=False
    )
```

```python
import jax
import jax.numpy as jnp
from jax import lax
from jax.experimental import pallas as pl
from jax.experimental.pallas import tpu as pltpu
from jax.sharding import PartitionSpec as P

MESH = pl.DeviceIdType.MESH
F32, BF16 = jnp.float32, jnp.bfloat16
NZ, NT = 12, 16
NP = 2 * NZ
PARTS = 3
STEP = NP // PARTS
CHUNKS = 8


def nt(a, b):
    return lax.dot_general(a, b, (((1,), (1,)), ((), ())), preferred_element_type=F32)


def nn(a, b):
    return jnp.dot(a, b, preferred_element_type=F32)


def tn(a, b):
    return lax.dot_general(a, b, (((0,), (0,)), ((), ())), preferred_element_type=F32)


def flat(x):
    return x.reshape(-1, x.shape[-1])


def kernel(
    h_hbm, dw_hbm, enc_hbm, dec_hbm, cot_hbm,
    out_hbm, gh_hbm, gd_hbm,
    dwv, encv, decv, cotv, hv, mv,
    gterm, gslot, gfull, gsib,
    sterm, sslot, sfull, ssib,
    dterm, dslot, outv, ghv, gdv,
    lsem, wsem, osem, msend, mrecv, psend, precv, asend, arecv,
):
    dp, t = lax.axis_index("dp"), lax.axis_index("tensor")
    z, yh, c = dp // 4, (dp // 2) % 2, dp % 2
    place = z * 2 + yh
    yo = 1 - yh

    def along(k):
        return lax.rem(z + (k + NZ) % NZ, NZ)

    def device(k, yy):
        return ((along(k) * 2 + yy) * 2 + c, t)

    sibling = (dp + 1 - 2 * c, t)

    depth = dw_hbm.shape[0] // CHUNKS
    own = [
        pltpu.make_async_copy(enc_hbm, encv, lsem.at[0]),
        pltpu.make_async_copy(cot_hbm, cotv.at[c], lsem.at[1]),
        pltpu.make_async_copy(h_hbm, hv.at[c], lsem.at[2]),
        pltpu.make_async_copy(dec_hbm.at[:, 0], decv.at[0], lsem.at[3]),
        pltpu.make_async_copy(dec_hbm.at[:, 1], decv.at[1], lsem.at[4]),
    ]
    weights = [
        pltpu.make_async_copy(
            dw_hbm.at[pl.ds(i * depth, depth)], dwv.at[pl.ds(i * depth, depth)], wsem.at[i]
        )
        for i in range(CHUNKS)
    ]
    own[0].start()
    for copy in weights:
        copy.start()
    for copy in own[1:]:
        copy.start()

    barrier = pltpu.get_barrier_semaphore()
    near = (1, -1, 2, -2)
    greet = [sibling, device(0, yo)]
    greet += [device(k, yh) for k in near]
    greet += [device(k, yh) for k in (4, -4)]
    for who in greet:
        pl.semaphore_signal(barrier, inc=1, device_id=who, device_id_type=MESH)

    @pl.loop(1, NT)
    def _(k):
        pl.semaphore_signal(
            barrier, inc=1, device_id=(dp, lax.rem(t + k, NT)), device_id_type=MESH
        )

    own[0].wait()
    code = jnp.zeros((16, dwv.shape[1]), F32)
    for i in range(CHUNKS):
        cut = pl.ds(i * depth, depth)
        weights[i].wait()
        code += nn(encv[:, cut], dwv[cut, :])
    mv[c, place] = code.astype(BF16)

    pl.semaphore_wait(barrier, len(greet) + NT - 1)

    sent = []

    def pass_on(slot, *to):
        for who in to:
            copy = pltpu.make_async_remote_copy(
                src_ref=mv.at[c, slot], dst_ref=mv.at[c, slot],
                send_sem=msend.at[len(sent)], recv_sem=mrecv.at[slot],
                device_id=who, device_id_type=MESH,
            )
            copy.start()
            sent.append(copy)

    def arrived(slot):
        pltpu.make_async_copy(mv.at[c, slot], mv.at[c, slot], mrecv.at[slot]).wait()

    pairs = []

    def to_sibling(src, dst):
        i = len(pairs)
        copy = pltpu.make_async_remote_copy(
            src_ref=src, dst_ref=dst, send_sem=psend.at[i], recv_sem=precv.at[i],
            device_id=sibling, device_id_type=MESH,
        )
        copy.start()
        pairs.append(copy)
        return copy

    def scatter(term, slots, i):
        @pl.loop(1, NT)
        def _(k):
            who = lax.rem(t + k, NT)
            pltpu.make_async_remote_copy(
                src_ref=term.at[who], dst_ref=slots.at[k - 1],
                send_sem=asend.at[i], recv_sem=arecv.at[i],
                device_id=(dp, who), device_id_type=MESH,
            ).start()

    def gather(full, i):
        @pl.loop(1, NT)
        def _(k):
            pltpu.make_async_remote_copy(
                src_ref=full.at[t], dst_ref=full.at[t],
                send_sem=asend.at[i], recv_sem=arecv.at[i],
                device_id=(dp, lax.rem(t + k, NT)), device_id_type=MESH,
            ).start()

    def all_of(ref, sem):
        pltpu.make_async_copy(ref, ref, sem).wait()

    def reduce(term, slots, full, i):
        all_of(slots, arecv.at[i])
        total = term[t].astype(F32)
        for k in range(NT - 1):
            total += slots[k].astype(F32)
        full[t] = total.astype(BF16)
        gather(full, i + 1)

    def split(term, value):
        rows = value.shape[0] // 8
        for s in range(2):
            for r in range(8):
                term[8 * s + r] = value[r * rows:(r + 1) * rows, s * 128:(s + 1) * 128].astype(BF16)

    up, down = device(4, yh), device(-4, yh)
    one, two = (device(1, yh), device(-1, yh)), (device(2, yh), device(-2, yh))
    pass_on(place, device(0, yo), up, down, *one, *two)

    for copy in own[1:]:
        copy.wait()
    cot_pair = to_sibling(cotv.at[c], cotv.at[c])
    hid_pair = to_sibling(hv.at[c], hv.at[c])

    cot_pair.wait_recv()
    split(gterm, nt(flat(decv[c]), flat(cotv[...])))
    scatter(gterm, gslot, 0)

    turn = jnp.where(z // 4 == 1, NZ - 4, 4)
    first, second = lax.rem(z + turn, NZ) * 2, lax.rem(z + NZ - turn, NZ) * 2
    arrived(first + yh)
    pass_on(first + yh, device(0, yo), *one)
    arrived(z * 2 + yo)
    pass_on(z * 2 + yo, *one, *two)
    arrived(second + yh)
    pass_on(second + yh, device(0, yo), *one)
    pass_on(along(-4) * 2 + yh, two[0])
    arrived(first + yo)
    pass_on(first + yo, *one)
    arrived(second + yo)
    pass_on(second + yo, *one)
    pass_on(along(4) * 2 + yo, two[1])

    hid_pair.wait_recv()
    hidden_both = flat(hv[...])
    m_pairs = []

    def latent(n):
        for r in range(STEP // 2):
            @pl.when(lax.rem(z, 4) != r)
            def _():
                arrived(n * STEP + 2 * r)
                arrived(n * STEP + 2 * r + 1)

        rows = pl.ds(n * STEP, STEP)
        m_pairs.append(to_sibling(mv.at[c, rows], mv.at[c, rows]))
        split(sterm.at[n], nt(flat(mv[c, rows]), hidden_both))
        scatter(sterm.at[n], sslot.at[n], 2 + 2 * n)

    s_pairs = []

    def shared(n):
        all_of(sfull.at[n, pl.ds(0, NT - 1)], arecv.at[3 + 2 * n])
        s_pairs.append(to_sibling(sfull.at[n, pl.ds(8 * (1 - c), 8)], ssib.at[n]))

    def decoder_terms(n):
        gd = nn(flat(sfull[n, 0:8]), cotv[0]) + nn(flat(sfull[n, 8:16]), cotv[1])
        dterm[n * STEP:(n + 1) * STEP] = gd.astype(BF16).reshape(STEP, 16, -1)

        @pl.loop(n * STEP, (n + 1) * STEP)
        def _(who):
            @pl.when(who != place)
            def _():
                pltpu.make_async_remote_copy(
                    src_ref=dterm.at[who], dst_ref=dslot.at[lax.rem(who - place + NP, NP) - 1],
                    send_sem=asend.at[8], recv_sem=arecv.at[8],
                    device_id=(who * 2 + c, t), device_id_type=MESH,
                ).start()

    reduce(gterm, gslot, gfull, 0)
    latent(0)
    latent(1)
    reduce(sterm.at[0], sslot.at[0], sfull.at[0], 2)
    latent(2)
    reduce(sterm.at[1], sslot.at[1], sfull.at[1], 4)
    all_of(gfull.at[pl.ds(0, NT - 1)], arecv.at[1])
    g_pair = to_sibling(gfull.at[pl.ds(8 * (1 - c), 8)], gsib)
    shared(0)
    decoder_terms(0)
    reduce(sterm.at[2], sslot.at[2], sfull.at[2], 6)
    shared(1)
    decoder_terms(1)

    for copy in m_pairs:
        copy.wait_recv()
    g_pair.wait_recv()
    gh = tn(flat(gfull[pl.ds(8 * c, 8)]), flat(mv[c]))
    gh += tn(flat(gsib[...]), flat(mv[1 - c]))
    ghv[...] = gh.astype(BF16)
    gh_out = pltpu.make_async_copy(ghv, gh_hbm, osem.at[0])
    gh_out.start()

    shared(2)
    decoder_terms(2)
    for copy in s_pairs:
        copy.wait_recv()
    value = tn(flat(sfull[:, pl.ds(8 * c, 8)]), flat(decv[c]))
    value += tn(flat(ssib[...]), flat(decv[1 - c]))
    outv[...] = value.astype(BF16)
    out_out = pltpu.make_async_copy(outv, out_hbm, osem.at[1])
    out_out.start()

    all_of(dslot, arecv.at[8])
    total = dterm[place].astype(F32)
    for k in range(NP - 1):
        total += dslot[k].astype(F32)
    gdv[...] = total * (1.0 / 6144.0**0.5)
    gd_out = pltpu.make_async_copy(gdv, gd_hbm, osem.at[2])
    gd_out.start()

    for copy in sent:
        copy.wait_send()
    for copy in pairs:
        copy.wait_send()
    for i, ref in enumerate((gslot, gslot) + (sslot.at[0],) * 6 + (dslot,)):
        all_of(ref, asend.at[i])
    gh_out.wait()
    out_out.wait()
    gd_out.wait()


def write_out(a, b, c, a_out, b_out, c_out, sem):
    copies = [
        pltpu.make_async_copy(src, dst, sem.at[i])
        for i, (src, dst) in enumerate(((a, a_out), (b, b_out), (c, c_out)))
    ]
    for copy in copies:
        copy.start()
    for copy in copies:
        copy.wait()


def per_device(hidden, down_weight, encoder, decoder, cotangent):
    tokens, width = hidden.shape
    model = down_weight.shape[0]
    wide = decoder.shape[1]
    hbm = pl.BlockSpec(memory_space=pltpu.HBM)
    V, D = pltpu.VMEM, pltpu.SemaphoreType.DMA
    out_shape = (
        jax.ShapeDtypeStruct((tokens, wide), BF16),
        jax.ShapeDtypeStruct((tokens, width), BF16),
        jax.ShapeDtypeStruct((16, wide), F32),
    )

    results = pl.pallas_call(
        kernel,
        out_shape=out_shape,
        in_specs=[hbm] * 5,
        out_specs=(hbm,) * 3,
        scratch_shapes=[
            V((model, width), BF16),
            V((16, model), BF16),
            V((2, NP, 16, wide), BF16),
            V((2, tokens, wide), BF16),
            V((2, tokens, width), BF16),
            V((2, NP, 16, width), BF16),
            V((NT, 16 * PARTS, 128), BF16),
            V((NT - 1, 16 * PARTS, 128), BF16),
            V((NT, 16 * PARTS, 128), BF16),
            V((NT // 2, 16 * PARTS, 128), BF16),
            V((PARTS, NT, 16, 128), BF16),
            V((PARTS, NT - 1, 16, 128), BF16),
            V((PARTS, NT, 16, 128), BF16),
            V((PARTS, NT // 2, 16, 128), BF16),
            V((NP, 16, wide), BF16),
            V((NP - 1, 16, wide), BF16),
            V((tokens, wide), BF16),
            V((tokens, width), BF16),
            V((16, wide), F32),
            D((5,)), D((CHUNKS,)), D((3,)), D((NP - 1,)), D((NP,)), D((9,)), D((9,)), D((9,)), D((9,)),
        ],
        compiler_params=pltpu.CompilerParams(
            collective_id=0, has_side_effects=True, vmem_limit_bytes=56 * 2**20
        ),
        name="down_projection",
    )(hidden, down_weight, encoder.T, decoder.reshape(NP, 2, 16, wide), cotangent)

    return pl.pallas_call(
        write_out,
        out_shape=out_shape,
        in_specs=[pl.BlockSpec(memory_space=pltpu.VMEM)] * 3,
        out_specs=(hbm,) * 3,
        scratch_shapes=[D((3,))],
        name="write_out",
    )(*results)


def solution(mesh):
    in_specs = (
        P("dp", "tensor"),
        P(None, "tensor"),
        P(None, "dp"),
        P(None, "tensor"),
        P("dp", "tensor"),
    )
    out_specs = (P("dp", "tensor"), P("dp", "tensor"), P("dp", "tensor"))
    return jax.shard_map(
        per_device, mesh=mesh, in_specs=in_specs, out_specs=out_specs, check_vma=False
    )
```
